256 devices in a mesh: seq: 64 (over z, y_hi, x), head: 4 (over y_lo, core).
Axes of the slice: x: 4, y: 4 (y_hi: 2, y_lo: 2; y = y_hi * 2 + y_lo), z: 8, core: 2. Of those that a mesh axis runs over, the one named last changes fastest.
Arguments:
- queries: bfloat16 [32768, 4096], P('seq', 'head'), may hold values from -100 to 100
- keys: bfloat16 [32768, 1024], P('seq', 'head'), may hold values from -5 to 5
- values: bfloat16 [32768, 1024], P('seq', 'head'), may hold values from -6 to 6
- lengths: int32 [16], replicated, may hold values from 1 to 4096, 32768 in all
- out_weight: bfloat16 [4096, 4096], P('head'), may hold values from -0.125 to 0.125
Outputs:
- mixed: bfloat16 [32768, 4096], P('seq', 'head')
The draws below stay inside these ranges and needn't reach their ends.
Inputs may be any that keep to these rules, and one draw needn't show every extreme that they name: `lengths`: each document holds at least one token and the longest holds exactly 4096.
All inputs are finite; a program needn't handle non-finite values.
Results may differ from the reference program's by a relative error of at most 0.019.
Values may be sent and summed in bfloat16 or wider, within the bound.
A program may use at most 64 MiB of HBM per device.

```python
import math
import jax
import jax.numpy as jnp
import numpy as np
from jax import lax

D = 4096
QH = 32
KEY_VALUE_HEADS = 8
HEAD_WIDTH = 128
GROUP = 4
TOKENS = 32768
MOST = 4096
NDOCS = 16


def shared_keys(key):
    return jnp.clip(jax.random.normal(key, (TOKENS, KEY_VALUE_HEADS * HEAD_WIDTH), jnp.float32), -5.0, 5.0)


def draw_keys(key, part):
    base = shared_keys(key)
    return base.astype(jnp.bfloat16)


def draw_queries(key, part):
    key = jax.random.fold_in(key, 12)
    fresh = jax.random.normal(key, (TOKENS, QH * HEAD_WIDTH), jnp.float32)
    return jnp.clip(fresh, -5.0, 5.0).astype(jnp.bfloat16)


def raised(entries, key, source, target, blocks, factor):
    def block_of(position):
        return (jnp.arange(entries.shape[position]) // (entries.shape[position] // blocks)).reshape((-1,) + (1,) * (entries.ndim - 1 - position))

    one_side = jax.random.permutation(key, blocks)[block_of(target)]
    other_side = (block_of(target) + blocks // 2) % blocks
    return jnp.where((block_of(source) == one_side) | (block_of(source) == other_side), factor * entries, entries)


def levels(own_key, extent, cuts, smallest, top_value):
    factor_of, own = 1.0, jax.random.fold_in(own_key, 6)
    for axis_at, shards_of in cuts:
        draws = jnp.exp(jax.random.uniform(jax.random.fold_in(own, axis_at), (shards_of,), jnp.float32, smallest / len(cuts), top_value / len(cuts)))
        factor_of = factor_of * jnp.repeat(draws, extent[axis_at] // shards_of).reshape([-1 if axis == axis_at else 1 for axis in range(len(extent))])
    return factor_of


def split_up(count, total, most, skew):
    portions = [(1 << 20) // math.isqrt(rank ** skew) + 1 for rank in range(2, count + 1)]
    surplus, given = total - most - (count - 1), [1] * (count - 1)
    while surplus > 0:
        candidates = [i for i in range(count - 1) if given[i] < most]
        mass, left = sum([portions[i] for i in candidates]), surplus
        for i in candidates:
            extra = min(most - given[i], max(1, left * portions[i] // mass), surplus)
            given[i] = given[i] + extra
            surplus = surplus - extra
    return np.array([most] + given)


def ragged(own_key, count, total, bound, slope):
    if count == 2:
        one = jax.random.randint(own_key, (), max(1, total - bound), min(bound, total - 1) + 1)
        return jnp.stack([one, total - one])
    tallies = jnp.asarray(split_up(count, total, bound, slope), jnp.int32)
    twos = (count - 1) // 2
    source_of, sink = tallies[1:1 + 2 * twos:2], tallies[2:2 + 2 * twos:2]
    room = jnp.minimum(source_of - 1, bound - sink)
    passed = jax.random.randint(jax.random.fold_in(own_key, 1), (twos,), 0, 1 << 20) % (room + 1)
    tallies = tallies.at[1:1 + 2 * twos:2].set(source_of - passed).at[2:2 + 2 * twos:2].set(sink + passed)
    return tallies[jax.random.permutation(jax.random.fold_in(own_key, 2), count)]


def gaussian(rng, shape, deviation, most, shards=(), held_as=jnp.bfloat16):
    result = jax.random.normal(rng, shape, jnp.float32) * deviation
    if len(shards) > 0:
        result = levels(rng, shape, shards, -0.22, 0.18) * result
    return jnp.clip(result, min=-most, max=most).astype(held_as)


def bell_draw_with(own_key, dims, deviation, bound, cuts, heavy, kind=jnp.bfloat16):
    values = deviation * jax.random.normal(own_key, dims, jnp.float32)
    if cuts:
        values = values * levels(own_key, dims, cuts, -0.22, 0.18)
    return jnp.clip(raised(values, jax.random.fold_in(own_key, 3), *heavy), -bound, bound).astype(kind)


def setup_inputs(seed: int = 0) -> dict:
    key_list = jax.random.split(jax.random.key(seed), 6)
    queries = draw_queries(jax.random.fold_in(key_list[5], 71), 0)
    keys = draw_keys(jax.random.fold_in(key_list[5], 71), 0)
    values = gaussian(key_list[2], (TOKENS, KEY_VALUE_HEADS * HEAD_WIDTH), 1.0, 6.0, ((0, 64), (1, 4)))
    lengths = ragged(key_list[3], NDOCS, TOKENS, MOST, 2).astype(jnp.int32)
    out_weight = bell_draw_with(key_list[4], (QH * HEAD_WIDTH, D), (QH * HEAD_WIDTH) ** -0.5, 0.125, ((0, 4),), (0, 1, 4, 2.0))
    return dict(queries=queries, keys=keys, values=values, lengths=lengths, out_weight=out_weight)


def doc_ids(lengths, count):
    ends = jnp.cumsum(lengths).astype(jnp.int32)
    places = jnp.arange(count, dtype=jnp.int32)
    return lax.optimization_barrier(jnp.sum((ends[None, :] <= places[:, None]).astype(jnp.int32), axis=1)).astype(jnp.int32)

def reference(queries, keys, values, lengths, out_weight):
    docs = doc_ids(lengths, TOKENS)
    q_rows = min(512, TOKENS)
    causal_window = min(MOST + q_rows, TOKENS)

    def block(index):
        first = (index * q_rows).astype(jnp.int32)
        key_first_position = jnp.clip(first + q_rows - causal_window, 0, TOKENS - causal_window).astype(jnp.int32)
        qmat = lax.dynamic_slice_in_dim(queries, first, q_rows, 0).astype(jnp.float32).reshape(q_rows, KEY_VALUE_HEADS, GROUP, HEAD_WIDTH)
        kmat = lax.dynamic_slice_in_dim(keys, key_first_position, causal_window, 0).astype(jnp.float32).reshape(causal_window, KEY_VALUE_HEADS, HEAD_WIDTH)
        value_matrix = lax.dynamic_slice_in_dim(values, key_first_position, causal_window, 0).astype(jnp.float32).reshape(causal_window, KEY_VALUE_HEADS, HEAD_WIDTH)
        q_pos = first + jnp.arange(q_rows, dtype=jnp.int32)
        k_pos = key_first_position + jnp.arange(causal_window, dtype=jnp.int32)
        q_doc = lax.dynamic_slice_in_dim(docs, first, q_rows, 0)
        k_doc = lax.dynamic_slice_in_dim(docs, key_first_position, causal_window, 0)
        allowed = (q_doc[:, None] == k_doc[None, :]) & (k_pos[None, :] <= q_pos[:, None])
        scores = jnp.einsum('qgrd,kgd->grqk', qmat, kmat) / math.sqrt(HEAD_WIDTH)
        scores = jnp.where(allowed, scores, -jnp.inf)
        top = lax.optimization_barrier(jnp.max(scores, axis=-1, keepdims=True))
        expo = jnp.exp(scores - top)
        total = lax.optimization_barrier(jnp.sum(expo, axis=-1))
        rounded_length = lax.optimization_barrier(expo.astype(jnp.bfloat16))
        numerator = jnp.einsum('zmcp,pzf->czmf', rounded_length.astype(jnp.float32), value_matrix)
        outs = numerator / jnp.transpose(total, (2, 0, 1))[..., None]
        return outs.astype(jnp.bfloat16).reshape(q_rows, QH * HEAD_WIDTH)
    attended = lax.map(block, jnp.arange(TOKENS // q_rows, dtype=jnp.int32)).reshape(TOKENS, QH * HEAD_WIDTH)
    return jnp.dot(attended, out_weight, preferred_element_type=jnp.float32).astype(jnp.bfloat16)
```

```python
import functools
import math

import jax
import jax.numpy as jnp
from jax import lax
from jax.experimental import pallas as pl
from jax.experimental.pallas import tpu as pltpu
from jax.sharding import PartitionSpec as P

HEAD = 128
GROUP = 4
ROWS = 512
BLOCK = 4 * ROWS
WINDOW = 3 * BLOCK
TILE = 512
DOCS = 16
STEPS = 8
SCALE = math.log2(math.e) / math.sqrt(HEAD)
LOW = -1e30
MESH = pl.DeviceIdType.MESH
NT = (((1,), (1,)), ((), ()))
ORDER = (0, 1, 3, 2)


def kernel(
    len_ref, q_hbm, k_hbm, v_hbm, w_hbm, out_ref,
    v_loc, vt, w, kv, q, thr, scores, acc, att_out, att, near_out, near_in,
    cross_out, cross_in, part, own,
    load_sem, kv_send, kv_recv, q_send, q_recv, z_send, z_recv, y_send, y_recv,
    sib_send, sib_recv, att_send, att_recv, near_send, near_recv, cross_send, cross_recv,
):
    s = lax.axis_index("seq")
    h = lax.axis_index("head")
    x = lax.rem(s, 4)
    yh = lax.rem(s // 4, 2)
    z = s // 8
    depth = lax.axis_size("seq") // 8
    yl = h // 2
    c = lax.rem(h, 2)

    def at(x_, c_):
        return (z * 8 + yh * 4 + x_, yl * 2 + c_)

    sibling = at(x, 1 - c)
    above = (lax.rem(z + 1, depth) * 8 + yh * 4 + x, h)
    below = (lax.rem(z + depth - 1, depth) * 8 + yh * 4 + x, h)
    across = (z * 8 + (1 - yh) * 4 + x, h)
    facing = (s, (1 - yl) * 2 + c)

    v_copy = pltpu.make_async_copy(v_hbm, v_loc, load_sem.at[0])
    w_copy = pltpu.make_async_copy(w_hbm, w, load_sem.at[1])
    v_copy.start()
    w_copy.start()

    barrier = pltpu.get_barrier_semaphore()
    partners = [sibling, above, below, across, facing]
    for d in (1, 2, 3):
        for e in (0, 1):
            partners.append(at(lax.rem(x + d, 4), e))
    for partner in partners:
        pl.semaphore_signal(barrier, inc=1, device_id=partner, device_id_type=MESH)

    n_at = lax.broadcasted_iota(jnp.int32, (STEPS, HEAD), 0)
    r_at = lax.broadcasted_iota(jnp.int32, (STEPS, HEAD), 1)
    begin = (s // 4) * BLOCK
    place = begin + (3 - (n_at & 3)) * ROWS + (n_at >> 2) * 256 + c * HEAD + r_at
    end = jnp.int32(0)
    start = jnp.zeros((STEPS, HEAD), jnp.int32)
    for d in range(DOCS):
        end = end + len_ref[d]
        start = jnp.where(place >= end, end, start)
    thr[...] = start - (begin - 2 * BLOCK)

    v_copy.wait()
    for i in range(2):
        for b in range(4):
            piece = v_loc[b * 128:(b + 1) * 128, i * 128:(i + 1) * 128]
            vt[i, b * 128:(b + 1) * 128, :] = piece.astype(jnp.float32).T.astype(jnp.bfloat16)

    pl.semaphore_wait(barrier, len(partners))

    def remote(src, dst, send, recv, device):
        return pltpu.make_async_remote_copy(
            src_ref=src, dst_ref=dst, send_sem=send, recv_sem=recv,
            device_id=device, device_id_type=MESH,
        )

    def each_way(is_self, copy, src, dst, recv):
        @pl.when(is_self)
        def _():
            pltpu.make_async_copy(src, dst, recv).start()

        @pl.when(jnp.logical_not(is_self))
        def _():
            copy.start()

    def arrived(dst, recv):
        pltpu.make_async_copy(dst, dst, recv).wait()

    def kv_at(kind, slot, shard):
        return kv.at[kind, pl.ds(pl.multiple_of(slot * BLOCK + shard * ROWS, ROWS), ROWS)]

    exchanged = []
    for kind in range(2):
        for i in range(2):
            src = k_hbm.at[:, pl.ds(i * HEAD, HEAD)] if kind == 0 else vt.at[i]
            dst = kv_at(kind, 2, x)
            is_self = (2 * c + i == x) & (c == kind)
            copy = remote(src, dst, kv_send.at[kind, i], kv_recv.at[x], at(2 * c + i, kind))
            each_way(is_self, copy, src, dst, kv_recv.at[x])
            exchanged.append((is_self, copy))
    for half in range(2):
        for i in range(2):
            for e in range(2):
                src = q_hbm.at[pl.ds(half * 256 + e * HEAD, HEAD), pl.ds(i * 512, 512)]
                step = half * 4 + 3 - x
                dst = q.at[step]
                is_self = (2 * c + i == x) & (c == e)
                copy = remote(src, dst, q_send.at[half, i, e], q_recv.at[step], at(2 * c + i, e))
                each_way(is_self, copy, src, dst, q_recv.at[step])
                exchanged.append((is_self, copy))

    def to_sibling(slot, shard):
        ref = kv_at(c, slot, shard)
        return remote(ref, ref, sib_send.at[slot, shard], sib_recv.at[slot, shard], sibling)

    def to_above(shard):
        return remote(kv_at(c, 2, shard), kv_at(c, 0, shard), z_send.at[shard], z_recv.at[shard], above)

    def to_across(slot, shard):
        return remote(kv_at(c, slot, shard), kv_at(c, 1, shard), y_send.at[shard], y_recv.at[shard], across)

    shards = [lax.rem(x + o, 4) for o in ORDER]
    for shard in shards:
        arrived(kv_at(c, 2, shard), kv_recv.at[shard])
        to_above(shard).start()

        @pl.when(yh == 0)
        def _():
            to_across(2, shard).start()

        to_sibling(2, shard).start()
    for shard in shards:
        arrived(kv_at(c, 0, shard), z_recv.at[shard])

        @pl.when(yh == 1)
        def _():
            to_across(0, shard).start()

        to_sibling(0, shard).start()
    for shard in shards:
        arrived(kv_at(c, 1, shard), y_recv.at[shard])
        to_sibling(1, shard).start()
    for slot in (2, 0, 1):
        for shard in shards:
            arrived(kv_at(1 - c, slot, shard), sib_recv.at[slot, shard])

    ones = jnp.ones((16, TILE), jnp.bfloat16)

    def attend(n):
        half = n // 4
        t = 3 - lax.rem(n, 4)
        low = pl.multiple_of(t * ROWS + half * 256 + c * HEAD, HEAD)
        arrived(q.at[n], q_recv.at[n])
        from_ = thr[pl.ds(n, 1), :]

        def weigh(off, count):
            q_all = jnp.concatenate([q[n, :, g * HEAD:(g + 1) * HEAD] for g in range(GROUP)], axis=0)
            return lax.dot_general(
                kv[0, pl.ds(off, count), :], q_all, NT, preferred_element_type=jnp.float32
            )

        def mix(off, count, p):
            blocks = [kv[1, pl.ds(pl.multiple_of(off + b * 128, 128), 128), :] for b in range(count // 128)]
            v_all = blocks[0] if len(blocks) == 1 else jnp.concatenate(blocks, axis=1)
            v_all = jnp.concatenate([v_all, ones[:, :count]], axis=0)
            return jnp.dot(v_all, p, preferred_element_type=jnp.float32)

        def masked(raw, allowed):
            bias = jnp.where(allowed, 0.0, LOW)
            return jnp.concatenate(
                [raw[:, g * HEAD:(g + 1) * HEAD] + bias for g in range(GROUP)], axis=1
            )

        diag = pl.multiple_of(low + 2 * BLOCK, HEAD)
        key_at = lax.broadcasted_iota(jnp.int32, (HEAD, HEAD), 0)
        row_at = lax.broadcasted_iota(jnp.int32, (HEAD, HEAD), 1)
        first = masked(weigh(diag, HEAD), (key_at <= row_at) & (key_at >= from_ - diag))
        top = jnp.max(first, axis=0, keepdims=True)
        acc[...] = mix(diag, HEAD, jnp.exp2((first - top) * SCALE).astype(jnp.bfloat16))

        def fill(slot, tile):
            off = pl.multiple_of(jnp.minimum(low + tile * TILE, WINDOW - TILE), HEAD)
            at_ = lax.broadcasted_iota(jnp.int32, (TILE, HEAD), 0)
            scores[slot] = masked(weigh(off, TILE), at_ >= from_ - off)

        fill(0, 0)

        def body(j, top):
            for u in range(4):
                tile = 4 * j + u
                fill((u + 1) % 2, tile + 1)
                now = scores[u % 2]
                new_top = jnp.maximum(top, jnp.max(now, axis=0, keepdims=True))
                p = jnp.exp2((now - new_top) * SCALE).astype(jnp.bfloat16)
                shrink = jnp.exp2((top - new_top) * SCALE)
                top = new_top
                off = pl.multiple_of(low + tile * TILE, HEAD)
                acc[...] = acc[...] * shrink + mix(off, TILE, p)
            return top

        lax.fori_loop(0, 2, body, top)
        done = acc[:HEAD] / acc[HEAD:HEAD + 1]
        for g in range(GROUP):
            att_out[n, :, g * HEAD:(g + 1) * HEAD] = done[:, g * HEAD:(g + 1) * HEAD].T.astype(jnp.bfloat16)

    def give_back(n):
        half = n // 4
        t = 3 - lax.rem(n, 4)
        dst = att.at[
            half,
            pl.ds(pl.multiple_of(c * HEAD, HEAD), HEAD),
            pl.ds(pl.multiple_of(lax.rem(x, 2) * 512, 512), 512),
        ]
        recv = att_recv.at[half, lax.rem(x, 2), c]
        copy = remote(att_out.at[n], dst, att_send.at[n], recv, at(t, x // 2))
        return (t == x) & (x // 2 == c), copy, att_out.at[n], dst, recv

    def near(half, which):
        return remote(
            near_out.at[half, which], near_in.at[half, which],
            near_send.at[half, which], near_recv.at[half, which], sibling,
        )

    def cross(half):
        return remote(
            cross_out.at[half], cross_in.at[half], cross_send.at[half], cross_recv.at[half], facing
        )

    def quarter(half, k, into):
        def body(j, carry):
            col = pl.multiple_of(k * 1024 + j * 512, 512)
            into(j * 512, jnp.dot(att[half], w[:, pl.ds(col, 512)], preferred_element_type=jnp.float32))
            return carry

        lax.fori_loop(0, 2, body, 0)

    def project(half):
        for e in range(2):
            for d in range(2):
                arrived(
                    att.at[half, pl.ds(d * HEAD, HEAD), pl.ds(e * 512, 512)], att_recv.at[half, e, d]
                )

        def to_near(which):
            def into(col, value):
                near_out[half, which, :, pl.ds(pl.multiple_of(col, 512), 512)] = value.astype(jnp.bfloat16)
            return into

        def to_part(col, value):
            part[:, pl.ds(pl.multiple_of(col, 512), 512)] = value

        def to_own(col, value):
            own[half, :, pl.ds(pl.multiple_of(col, 512), 512)] = value

        quarter(half, (1 - yl) * 2 + 1 - c, to_near(0))
        near(half, 0).start()
        quarter(half, (1 - yl) * 2 + c, to_part)
        near(half, 0).wait_recv()
        cross_out[half] = (part[...] + near_in[half, 0].astype(jnp.float32)).astype(jnp.bfloat16)
        cross(half).start()
        quarter(half, yl * 2 + 1 - c, to_near(1))
        near(half, 1).start()
        quarter(half, yl * 2 + c, to_own)

    w_copy.wait()

    def turn(n, carry):
        @pl.when(n < STEPS)
        def _():
            attend(n)
            is_self, copy, src, dst, recv = give_back(n)
            each_way(is_self, copy, src, dst, recv)

        late = n - (4 - x)

        @pl.when((late == 0) | (late == 4))
        def _():
            project(late // 4)

        return carry

    lax.fori_loop(0, STEPS + 1, turn, 0)

    for half in range(2):
        near(half, 1).wait_recv()
        cross(half).wait_recv()
        out_ref[half * 256:(half + 1) * 256, :] = (
            own[half] + near_in[half, 1].astype(jnp.float32) + cross_in[half].astype(jnp.float32)
        ).astype(jnp.bfloat16)

    for is_self, copy in exchanged:
        @pl.when(jnp.logical_not(is_self))
        def _():
            copy.wait_send()

    for shard in range(4):
        to_above(shard).wait_send()
        to_across(0, shard).wait_send()
        for slot in range(3):
            to_sibling(slot, shard).wait_send()
    for n in range(STEPS):
        is_self, copy, _, _, _ = give_back(n)

        @pl.when(jnp.logical_not(is_self))
        def _():
            copy.wait_send()

    for half in range(2):
        near(half, 0).wait_send()
        near(half, 1).wait_send()
        cross(half).wait_send()


def on_device(queries, keys, values, lengths, out_weight):
    bf16, f32 = jnp.bfloat16, jnp.float32
    dma = pltpu.SemaphoreType.DMA
    anywhere = pl.BlockSpec(memory_space=pl.ANY)
    return pl.pallas_call(
        kernel,
        out_shape=jax.ShapeDtypeStruct((ROWS, 1024), bf16),
        in_specs=[pl.BlockSpec(memory_space=pltpu.SMEM)] + [anywhere] * 4,
        out_specs=pl.BlockSpec(memory_space=pltpu.VMEM),
        scratch_shapes=[
            pltpu.VMEM((ROWS, 256), bf16),
            pltpu.VMEM((2, ROWS, HEAD), bf16),
            pltpu.VMEM((1024, 4096), bf16),
            pltpu.VMEM((2, WINDOW, HEAD), bf16),
            pltpu.VMEM((STEPS, HEAD, 512), bf16),
            pltpu.VMEM((STEPS, HEAD), jnp.int32),
            pltpu.VMEM((2, TILE, 512), f32),
            pltpu.VMEM((HEAD + 16, 512), f32),
            pltpu.VMEM((STEPS, HEAD, 512), bf16),
            pltpu.VMEM((2, 256, 1024), bf16),
            pltpu.VMEM((2, 2, 256, 1024), bf16),
            pltpu.VMEM((2, 2, 256, 1024), bf16),
            pltpu.VMEM((2, 256, 1024), bf16),
            pltpu.VMEM((2, 256, 1024), bf16),
            pltpu.VMEM((256, 1024), f32),
            pltpu.VMEM((2, 256, 1024), f32),
            dma((2,)),
            dma((2, 2)), dma((4,)),
            dma((2, 2, 2)), dma((STEPS,)),
            dma((4,)), dma((4,)),
            dma((4,)), dma((4,)),
            dma((3, 4)), dma((3, 4)),
            dma((STEPS,)), dma((2, 2, 2)),
            dma((2, 2)), dma((2, 2)),
            dma((2,)), dma((2,)),
        ],
        compiler_params=pltpu.CompilerParams(
            collective_id=0, has_side_effects=True, vmem_limit_bytes=56 * 2**20
        ),
        name="attend_and_project",
    )(lengths, queries, keys, values, out_weight)


def solution(mesh):
    in_specs = (P("seq", "head"), P("seq", "head"), P("seq", "head"), P(), P("head", None))
    return jax.shard_map(
        on_device, mesh=mesh, in_specs=in_specs, out_specs=P("seq", "head"), check_vma=False
    )
```

```python
import functools
import math

import jax
import jax.numpy as jnp
from jax import lax
from jax.experimental import pallas as pl
from jax.experimental.pallas import tpu as pltpu
from jax.sharding import PartitionSpec as P

HEAD = 128
GROUP = 4
ROWS = 512
BLOCK = 4 * ROWS
WINDOW = 3 * BLOCK
TILE = 512
DOCS = 16
STEPS = 8
PART = 128
SCALE = math.log2(math.e) / math.sqrt(HEAD)
LOW = -1e30
MESH = pl.DeviceIdType.MESH
NT = (((1,), (1,)), ((), ()))
ORDER = (0, 1, 3, 2)


def kernel(
    len_ref, q_hbm, k_hbm, v_hbm, w_hbm, out_hbm,
    out_loc, v_loc, vt, w, kv, q, thr, scores, acc, tops, att_out, att, near_out, near_in,
    cross_out, cross_in, part, own,
    load_sem, kv_send, kv_recv, q_send, q_recv, z_send, z_recv, y_send, y_recv,
    sib_send, sib_recv, att_send, att_recv, near_send, near_recv, cross_send, cross_recv, out_sem,
):
    s = lax.axis_index("seq")
    h = lax.axis_index("head")
    x = lax.rem(s, 4)
    yh = lax.rem(s // 4, 2)
    z = s // 8
    depth = lax.axis_size("seq") // 8
    yl = h // 2
    c = lax.rem(h, 2)

    def at(x_, c_):
        return (z * 8 + yh * 4 + x_, yl * 2 + c_)

    sibling = at(x, 1 - c)
    above = (lax.rem(z + 1, depth) * 8 + yh * 4 + x, h)
    below = (lax.rem(z + depth - 1, depth) * 8 + yh * 4 + x, h)
    across = (z * 8 + (1 - yh) * 4 + x, h)
    facing = (s, (1 - yl) * 2 + c)

    v_copy = pltpu.make_async_copy(v_hbm, v_loc, load_sem.at[0])
    w_copy = pltpu.make_async_copy(w_hbm, w, load_sem.at[1])
    v_copy.start()
    w_copy.start()

    barrier = pltpu.get_barrier_semaphore()
    partners = [sibling, above, below, across, facing]
    for d in (1, 2, 3):
        for e in (0, 1):
            partners.append(at(lax.rem(x + d, 4), e))
    for partner in partners:
        pl.semaphore_signal(barrier, inc=1, device_id=partner, device_id_type=MESH)

    n_at = lax.broadcasted_iota(jnp.int32, (STEPS, HEAD), 0)
    r_at = lax.broadcasted_iota(jnp.int32, (STEPS, HEAD), 1)
    begin = (s // 4) * BLOCK
    place = begin + ((n_at & 1) * 2 + (r_at >> 6)) * ROWS + (n_at >> 1) * PART + c * 64 + (r_at & 63)
    end = jnp.int32(0)
    start = jnp.zeros((STEPS, HEAD), jnp.int32)
    for d in range(DOCS):
        end = end + len_ref[d]
        start = jnp.where(place >= end, end, start)
    thr[...] = start - (begin - 2 * BLOCK)

    v_copy.wait()
    for i in range(2):
        for b in range(4):
            piece = v_loc[b * 128:(b + 1) * 128, i * 128:(i + 1) * 128]
            vt[i, b * 128:(b + 1) * 128, :] = piece.astype(jnp.float32).T.astype(jnp.bfloat16)

    pl.semaphore_wait(barrier, len(partners))

    def remote(src, dst, send, recv, device):
        return pltpu.make_async_remote_copy(
            src_ref=src, dst_ref=dst, send_sem=send, recv_sem=recv,
            device_id=device, device_id_type=MESH,
        )

    def each_way(is_self, copy, src, dst, recv):
        @pl.when(is_self)
        def _():
            pltpu.make_async_copy(src, dst, recv).start()

        @pl.when(jnp.logical_not(is_self))
        def _():
            copy.start()

    def arrived(dst, recv):
        pltpu.make_async_copy(dst, dst, recv).wait()

    def kv_at(kind, slot, shard):
        return kv.at[kind, pl.ds(pl.multiple_of(slot * BLOCK + shard * ROWS, ROWS), ROWS)]

    exchanged = []
    distant = []
    for kind in range(2):
        for i in range(2):
            src = k_hbm.at[:, pl.ds(i * HEAD, HEAD)] if kind == 0 else vt.at[i]
            dst = kv_at(kind, 2, x)
            is_self = (c + 2 * i == x) & (c == kind)
            is_far = lax.rem(c + 2 * i + 6 - x, 4) == 0
            copy = remote(src, dst, kv_send.at[kind, i], kv_recv.at[x], at(c + 2 * i, kind))

            each_way(is_self, copy, src, dst, kv_recv.at[x])

            exchanged.append((is_self, copy))
            distant.append((is_far, copy))

    def send_queries(part_):
        for e in range(2):
            for i in range(2):
                src = q_hbm.at[pl.ds(part_ * PART + e * 64, 64), pl.ds(i * 512, 512)]
                which = part_ * 2 + x // 2
                dst = q.at[which, pl.ds(pl.multiple_of(lax.rem(x, 2) * 64, 64), 64)]
                recv = q_recv.at[which, lax.rem(x, 2)]
                is_self = (c + 2 * i == x) & (c == e)
                copy = remote(src, dst, q_send.at[part_, i, e], recv, at(c + 2 * i, e))
                each_way(is_self, copy, src, dst, recv)
                exchanged.append((is_self, copy))

    def to_sibling(slot, shard):
        ref = kv_at(c, slot, shard)
        return remote(ref, ref, sib_send.at[slot, shard], sib_recv.at[slot, shard], sibling)

    def to_above(shard):
        return remote(kv_at(c, 2, shard), kv_at(c, 0, shard), z_send.at[shard], z_recv.at[shard], above)

    def to_across(slot, shard):
        return remote(kv_at(c, slot, shard), kv_at(c, 1, shard), y_send.at[shard], y_recv.at[shard], across)

    shards = [lax.rem(x + o, 4) for o in ORDER]
    def pass_own(shard):
        arrived(kv_at(c, 2, shard), kv_recv.at[shard])
        to_above(shard).start()

        @pl.when(yh == 0)
        def _():
            to_across(2, shard).start()

        to_sibling(2, shard).start()

    for shard in shards:
        pass_own(shard)
    send_queries(0)
    for part_ in range(1, 4):
        send_queries(part_)

    def pass_below(shard):
        arrived(kv_at(c, 0, shard), z_recv.at[shard])

        @pl.when(yh == 1)
        def _():
            to_across(0, shard).start()

        to_sibling(0, shard).start()

    def pass_across(shard):
        arrived(kv_at(c, 1, shard), y_recv.at[shard])
        to_sibling(1, shard).start()

    def from_sibling(slot):
        for shard in shards:
            arrived(kv_at(1 - c, slot, shard), sib_recv.at[slot, shard])

    pass_below(shards[0])
    pass_below(shards[1])
    from_sibling(2)

    ones = jnp.ones((16, TILE), jnp.bfloat16)

    def step_of(n):
        return (n // 2) * 2 + lax.rem(x // 2 + 1 + lax.rem(n, 2), 2)

    def low_of(which):
        return pl.multiple_of(lax.rem(which, 2) * 2 * ROWS + (which // 2) * PART, PART)

    def weigh(which, off, count):
        q_all = jnp.concatenate([q[which, :, g * HEAD:(g + 1) * HEAD] for g in range(GROUP)], axis=0)
        return lax.dot_general(
            kv[0, pl.ds(off, count), :], q_all, NT, preferred_element_type=jnp.float32
        )

    def mix(off, count, p):
        blocks = [kv[1, pl.ds(pl.multiple_of(off + b * 128, 128), 128), :] for b in range(count // 128)]
        v_all = blocks[0] if len(blocks) == 1 else jnp.concatenate(blocks, axis=1)
        v_all = jnp.concatenate([v_all, ones[:, :count]], axis=0)
        return jnp.dot(v_all, p, preferred_element_type=jnp.float32)

    def masked(raw, allowed):
        bias = jnp.where(allowed, 0.0, LOW)
        return jnp.concatenate(
            [raw[:, g * HEAD:(g + 1) * HEAD] + bias for g in range(GROUP)], axis=1
        )

    def allowed_at(which, off, count, causal):
        key_at = lax.broadcasted_iota(jnp.int32, (count, HEAD), 0)
        allowed = key_at >= thr[pl.ds(which, 1), :] - off
        if causal:
            col = lax.broadcasted_iota(jnp.int32, (1, HEAD), 1)
            place = low_of(which) + 2 * BLOCK + c * 64 + (col >> 6) * ROWS + (col & 63)
            allowed = allowed & (key_at <= place - off)
        return allowed

    def fill(slot, which, tile, causal=False):
        off = pl.multiple_of(low_of(which) + tile * TILE, HEAD)
        scores[slot] = masked(weigh(which, off, TILE), allowed_at(which, off, TILE, causal))

    def fold(slot, which, tile, top):
        now = scores[slot]
        new_top = jnp.maximum(top, jnp.max(now, axis=0, keepdims=True))
        p = jnp.exp2((now - new_top) * SCALE).astype(jnp.bfloat16)
        shrink = jnp.exp2((top - new_top) * SCALE)
        off = pl.multiple_of(low_of(which) + tile * TILE, HEAD)
        acc[which] = acc[which] * shrink + mix(off, TILE, p)
        return new_top

    def begin_step(which, tiles, extra=()):
        for e in range(2):
            arrived(q.at[which, pl.ds(e * 64, 64)], q_recv.at[which, e])
        diag = pl.multiple_of(low_of(which) + 9 * TILE, HEAD)
        first = masked(weigh(which, diag, HEAD), allowed_at(which, diag, HEAD, True))
        jobs = [(which, tile) for tile in tiles] + list(extra)
        fill(0, which, tiles[0], True)
        top = jnp.max(first, axis=0, keepdims=True)
        acc[which] = mix(diag, HEAD, jnp.exp2((first - top) * SCALE).astype(jnp.bfloat16))
        for u, (one, tile) in enumerate(jobs):
            if u + 1 < len(jobs):
                fill((u + 1) % 2, *jobs[u + 1])
            if u == len(tiles):
                tops[which] = top
                top = tops[one]
            top = fold(u % 2, one, tile, top)
        tops[jobs[-1][0]] = top

    def end_step(n):
        which = step_of(n)
        then = step_of(jnp.minimum(n + 1, STEPS - 1))
        base = 3 - 2 * lax.rem(which, 2)
        top = tops[which]
        for u in range(5):
            if u < 4:
                fill(u % 2, which, base + u + 1)
            else:
                fill(2, then, 3 - 2 * lax.rem(then, 2))
            top = fold((u - 1) % 2 if u else 2, which, base + u, top)
        done = acc[which, :HEAD] / acc[which, HEAD:HEAD + 1]
        for g in range(GROUP):
            att_out[n, :, g * HEAD:(g + 1) * HEAD] = done[:, g * HEAD:(g + 1) * HEAD].T.astype(jnp.bfloat16)

    def give_back(n, e):
        which = step_of(n)
        t = 2 * lax.rem(which, 2) + e
        src = att_out.at[n, pl.ds(e * 64, 64)]
        dst = att.at[
            which // 2,
            pl.ds(pl.multiple_of(c * 64, 64), 64),
            pl.ds(pl.multiple_of((x // 2) * 512, 512), 512),
        ]
        recv = att_recv.at[which // 2, x // 2, c]
        copy = remote(src, dst, att_send.at[n, e], recv, at(t, lax.rem(x, 2)))
        return (t == x) & (lax.rem(x, 2) == c), copy, src, dst, recv

    def near(half, which):
        return remote(
            near_out.at[half, which], near_in.at[half, which],
            near_send.at[half, which], near_recv.at[half, which], sibling,
        )

    def cross(half):
        return remote(
            cross_out.at[half], cross_in.at[half], cross_send.at[half], cross_recv.at[half], facing
        )

    def quarter(half, k, into):
        col = pl.multiple_of(k * 1024, 1024)
        into(jnp.dot(att[half], w[:, pl.ds(col, 1024)], preferred_element_type=jnp.float32))

    def project(half):
        for e in range(2):
            for d in range(2):
                arrived(
                    att.at[half, pl.ds(d * 64, 64), pl.ds(e * 512, 512)], att_recv.at[half, e, d]
                )

        def to_near(which):
            def into(value):
                near_out[half, which] = value.astype(jnp.bfloat16)
            return into

        def to_part(value):
            part[half] = value

        def to_own(value):
            own[half] = value

        quarter(half, (1 - yl) * 2 + 1 - c, to_near(0))
        near(half, 0).start()
        quarter(half, (1 - yl) * 2 + c, to_part)
        quarter(half, yl * 2 + 1 - c, to_near(1))
        near(half, 1).start()
        quarter(half, yl * 2 + c, to_own)

    def combine(half):
        near(half, 0).wait_recv()
        cross_out[half] = (part[half] + near_in[half, 0].astype(jnp.float32)).astype(jnp.bfloat16)
        cross(half).start()

    def begin_far(a, carry):
        begin_step(2 * a + 1, (8, 7, 6))
        return carry

    def begin_near(a, carry):
        begin_step(2 * a, (8, 2, 1, 0), ((2 * a + 1, 0),))
        return carry

    lax.fori_loop(0, 2, begin_far, 0)
    pass_below(shards[2])
    pass_below(shards[3])
    lax.fori_loop(2, 4, begin_far, 0)
    from_sibling(0)
    lax.fori_loop(0, 2, begin_near, 0)
    for shard in shards:
        pass_across(shard)
    lax.fori_loop(2, 4, begin_near, 0)
    from_sibling(1)
    w_copy.wait()
    fill(2, step_of(0), 3 - 2 * lax.rem(step_of(0), 2))

    def turn(n, carry):
        end_step(n)
        for e in range(2):
            is_self, copy, src, dst, recv = give_back(n, e)
            each_way(is_self, copy, src, dst, recv)

        @pl.when((lax.rem(n, 2) == 0) & (n > 0))
        def _():
            project(n // 2 - 1)

        @pl.when((lax.rem(n, 2) == 1) & (n > 1))
        def _():
            combine(n // 2 - 1)

        return carry

    lax.fori_loop(0, STEPS, turn, 0)
    project(3)
    combine(3)

    def out_copy(half):
        rows = pl.ds(half * PART, PART)
        return pltpu.make_async_copy(out_loc.at[rows], out_hbm.at[rows], out_sem.at[half])

    for half in range(4):
        near(half, 1).wait_recv()
        cross(half).wait_recv()
        out_loc[half * PART:(half + 1) * PART, :] = (
            own[half] + near_in[half, 1].astype(jnp.float32) + cross_in[half].astype(jnp.float32)
        ).astype(jnp.bfloat16)
        out_copy(half).start()

    for is_self, copy in exchanged:
        @pl.when(jnp.logical_not(is_self))
        def _():
            copy.wait_send()

    for shard in range(4):
        to_above(shard).wait_send()
        to_across(0, shard).wait_send()
        for slot in range(3):
            to_sibling(slot, shard).wait_send()
    for n in range(STEPS):
        for e in range(2):
            is_self, copy, _, _, _ = give_back(n, e)

            @pl.when(jnp.logical_not(is_self))
            def _():
                copy.wait_send()

    for half in range(4):
        out_copy(half).wait()
        near(half, 0).wait_send()
        near(half, 1).wait_send()
        cross(half).wait_send()


def on_device(queries, keys, values, lengths, out_weight):
    bf16, f32 = jnp.bfloat16, jnp.float32
    dma = pltpu.SemaphoreType.DMA
    anywhere = pl.BlockSpec(memory_space=pl.ANY)
    return pl.pallas_call(
        kernel,
        out_shape=jax.ShapeDtypeStruct((ROWS, 1024), bf16),
        in_specs=[pl.BlockSpec(memory_space=pltpu.SMEM)] + [anywhere] * 4,
        out_specs=anywhere,
        scratch_shapes=[
            pltpu.VMEM((ROWS, 1024), bf16),
            pltpu.VMEM((ROWS, 256), bf16),
            pltpu.VMEM((2, ROWS, HEAD), bf16),
            pltpu.VMEM((1024, 4096), bf16),
            pltpu.VMEM((2, WINDOW, HEAD), bf16),
            pltpu.VMEM((STEPS, HEAD, 512), bf16),
            pltpu.VMEM((STEPS, HEAD), jnp.int32),
            pltpu.VMEM((3, TILE, 512), f32),
            pltpu.VMEM((STEPS, HEAD + 16, 512), f32),
            pltpu.VMEM((STEPS, 1, 512), f32),
            pltpu.VMEM((STEPS, HEAD, 512), bf16),
            pltpu.VMEM((4, PART, 1024), bf16),
            pltpu.VMEM((4, 2, PART, 1024), bf16),
            pltpu.VMEM((4, 2, PART, 1024), bf16),
            pltpu.VMEM((4, PART, 1024), bf16),
            pltpu.VMEM((4, PART, 1024), bf16),
            pltpu.VMEM((4, PART, 1024), f32),
            pltpu.VMEM((4, PART, 1024), f32),
            dma((2,)),
            dma((2, 2)), dma((4,)),
            dma((4, 2, 2)), dma((STEPS, 2)),
            dma((4,)), dma((4,)),
            dma((4,)), dma((4,)),
            dma((3, 4)), dma((3, 4)),
            dma((STEPS, 2)), dma((4, 2, 2)),
            dma((4, 2)), dma((4, 2)),
            dma((4,)), dma((4,)), dma((4,)),
        ],
        compiler_params=pltpu.CompilerParams(
            collective_id=0, has_side_effects=True, vmem_limit_bytes=56 * 2**20
        ),
        name="attend_and_project",
    )(lengths, queries, keys, values, out_weight)


def solution(mesh):
    in_specs = (P("seq", "head"), P("seq", "head"), P("seq", "head"), P(), P("head", None))
    return jax.shard_map(
        on_device, mesh=mesh, in_specs=in_specs, out_specs=P("seq", "head"), check_vma=False
    )
```

```python
import functools
import math

import jax
import jax.numpy as jnp
from jax import lax
from jax.experimental import pallas as pl
from jax.experimental.pallas import tpu as pltpu
from jax.sharding import PartitionSpec as P

HEAD = 128
GROUP = 4
ROWS = 512
BLOCK = 4 * ROWS
WINDOW = 3 * BLOCK
TILE = 512
DOCS = 16
STEPS = 8
PART = 128
SCALE = math.log2(math.e) / math.sqrt(HEAD)
LOW = -1e30
MESH = pl.DeviceIdType.MESH
NT = (((1,), (1,)), ((), ()))
ORDER = (0, 1, 3, 2)


def kernel(
    len_ref, q_hbm, k_hbm, v_hbm, w_hbm, out_hbm,
    out_loc, v_loc, vt, w, kv, q, thr, scores, acc, tops, att_out, att, near_out, near_in,
    cross_out, cross_in, part, own,
    load_sem, kv_send, kv_recv, q_send, q_recv, z_send, z_recv, y_send, y_recv,
    sib_send, sib_recv, att_send, att_recv, near_send, near_recv, cross_send, cross_recv, out_sem,
):
    s = lax.axis_index("seq")
    h = lax.axis_index("head")
    x = lax.rem(s, 4)
    yh = lax.rem(s // 4, 2)
    z = s // 8
    depth = lax.axis_size("seq") // 8
    yl = h // 2
    c = lax.rem(h, 2)

    def at(x_, c_):
        return (z * 8 + yh * 4 + x_, yl * 2 + c_)

    sibling = at(x, 1 - c)
    above = (lax.rem(z + 1, depth) * 8 + yh * 4 + x, h)
    below = (lax.rem(z + depth - 1, depth) * 8 + yh * 4 + x, h)
    across = (z * 8 + (1 - yh) * 4 + x, h)
    facing = (s, (1 - yl) * 2 + c)

    v_copy = pltpu.make_async_copy(v_hbm, v_loc, load_sem.at[0])
    w_copy = pltpu.make_async_copy(w_hbm, w, load_sem.at[1])
    v_copy.start()
    w_copy.start()

    barrier = pltpu.get_barrier_semaphore()
    partners = [sibling, above, below, across, facing]
    for d in (1, 2, 3):
        for e in (0, 1):
            partners.append(at(lax.rem(x + d, 4), e))
    for partner in partners:
        pl.semaphore_signal(barrier, inc=1, device_id=partner, device_id_type=MESH)

    n_at = lax.broadcasted_iota(jnp.int32, (STEPS, HEAD), 0)
    r_at = lax.broadcasted_iota(jnp.int32, (STEPS, HEAD), 1)
    begin = (s // 4) * BLOCK
    place = begin + ((n_at & 1) * 2 + (r_at >> 6)) * ROWS + (n_at >> 1) * PART + c * 64 + (r_at & 63)
    end = jnp.int32(0)
    start = jnp.zeros((STEPS, HEAD), jnp.int32)
    for d in range(DOCS):
        end = end + len_ref[d]
        start = jnp.where(place >= end, end, start)
    thr[...] = start - (begin - 2 * BLOCK)

    v_copy.wait()
    for i in range(2):
        for b in range(4):
            piece = v_loc[b * 128:(b + 1) * 128, i * 128:(i + 1) * 128]
            vt[i, b * 128:(b + 1) * 128, :] = piece.astype(jnp.float32).T.astype(jnp.bfloat16)

    pl.semaphore_wait(barrier, len(partners))

    def remote(src, dst, send, recv, device):
        return pltpu.make_async_remote_copy(
            src_ref=src, dst_ref=dst, send_sem=send, recv_sem=recv,
            device_id=device, device_id_type=MESH,
        )

    def each_way(is_self, copy, src, dst, recv):
        @pl.when(is_self)
        def _():
            pltpu.make_async_copy(src, dst, recv).start()

        @pl.when(jnp.logical_not(is_self))
        def _():
            copy.start()

    def arrived(dst, recv):
        pltpu.make_async_copy(dst, dst, recv).wait()

    def kv_at(kind, slot, shard):
        return kv.at[kind, pl.ds(pl.multiple_of(slot * BLOCK + shard * ROWS, ROWS), ROWS)]

    exchanged = []
    distant = []
    for kind in range(2):
        for i in range(2):
            src = k_hbm.at[:, pl.ds(i * HEAD, HEAD)] if kind == 0 else vt.at[i]
            dst = kv_at(kind, 2, x)
            is_self = (c + 2 * i == x) & (c == kind)
            is_far = lax.rem(c + 2 * i + 6 - x, 4) == 0
            copy = remote(src, dst, kv_send.at[kind, i], kv_recv.at[x], at(c + 2 * i, kind))

            each_way(is_self, copy, src, dst, kv_recv.at[x])

            exchanged.append((is_self, copy))
            distant.append((is_far, copy))

    def send_queries(part_):
        for e in range(2):
            for i in range(2):
                src = q_hbm.at[pl.ds(part_ * PART + e * 64, 64), pl.ds(i * 512, 512)]
                which = part_ * 2 + x // 2
                dst = q.at[which, pl.ds(pl.multiple_of(lax.rem(x, 2) * 64, 64), 64)]
                recv = q_recv.at[which, lax.rem(x, 2)]
                is_self = (c + 2 * i == x) & (c == e)
                copy = remote(src, dst, q_send.at[part_, i, e], recv, at(c + 2 * i, e))
                each_way(is_self, copy, src, dst, recv)
                exchanged.append((is_self, copy))

    def to_sibling(slot, shard):
        ref = kv_at(c, slot, shard)
        return remote(ref, ref, sib_send.at[slot, shard], sib_recv.at[slot, shard], sibling)

    def to_above(shard):
        return remote(kv_at(c, 2, shard), kv_at(c, 0, shard), z_send.at[shard], z_recv.at[shard], above)

    def to_across(slot, shard):
        return remote(kv_at(c, slot, shard), kv_at(c, 1, shard), y_send.at[shard], y_recv.at[shard], across)

    shards = [lax.rem(x + o, 4) for o in ORDER]
    def pass_own(shard):
        arrived(kv_at(c, 2, shard), kv_recv.at[shard])
        to_above(shard).start()

        @pl.when(yh == 0)
        def _():
            to_across(2, shard).start()

        to_sibling(2, shard).start()

    for shard in shards:
        pass_own(shard)
    send_queries(0)
    for part_ in range(1, 4):
        send_queries(part_)

    def pass_below(shard):
        arrived(kv_at(c, 0, shard), z_recv.at[shard])

        @pl.when(yh == 1)
        def _():
            to_across(0, shard).start()

        to_sibling(0, shard).start()

    def pass_across(shard):
        arrived(kv_at(c, 1, shard), y_recv.at[shard])
        to_sibling(1, shard).start()

    def from_sibling(slot):
        for shard in shards:
            arrived(kv_at(1 - c, slot, shard), sib_recv.at[slot, shard])

    pass_below(shards[0])
    pass_below(shards[1])
    from_sibling(2)

    ones = jnp.ones((16, TILE), jnp.bfloat16)

    def step_of(n):
        return (n // 2) * 2 + lax.rem(x // 2 + 1 + lax.rem(n, 2), 2)

    def low_of(which):
        return pl.multiple_of(lax.rem(which, 2) * 2 * ROWS + (which // 2) * PART, PART)

    def weigh(which, off, count):
        q_all = jnp.concatenate([q[which, :, g * HEAD:(g + 1) * HEAD] for g in range(GROUP)], axis=0)
        return lax.dot_general(
            kv[0, pl.ds(off, count), :], q_all, NT, preferred_element_type=jnp.float32
        )

    def mix(off, count, p):
        blocks = [kv[1, pl.ds(pl.multiple_of(off + b * 128, 128), 128), :] for b in range(count // 128)]
        v_all = blocks[0] if len(blocks) == 1 else jnp.concatenate(blocks, axis=1)
        v_all = jnp.concatenate([v_all, ones[:, :count]], axis=0)
        return jnp.dot(v_all, p, preferred_element_type=jnp.float32)

    def masked(raw, allowed):
        bias = jnp.where(allowed, 0.0, LOW)
        return jnp.concatenate(
            [raw[:, g * HEAD:(g + 1) * HEAD] + bias for g in range(GROUP)], axis=1
        )

    def allowed_at(which, off, count, causal):
        key_at = lax.broadcasted_iota(jnp.int32, (count, HEAD), 0)
        allowed = key_at >= thr[pl.ds(which, 1), :] - off
        if causal:
            col = lax.broadcasted_iota(jnp.int32, (1, HEAD), 1)
            place = low_of(which) + 2 * BLOCK + c * 64 + (col >> 6) * ROWS + (col & 63)
            allowed = allowed & (key_at <= place - off)
        return allowed

    def fill(slot, which, tile, causal=False):
        off = pl.multiple_of(low_of(which) + tile * TILE, HEAD)
        scores[slot] = masked(weigh(which, off, TILE), allowed_at(which, off, TILE, causal))

    def fold(slot, which, tile, top):
        now = scores[slot]
        new_top = jnp.maximum(top, jnp.max(now, axis=0, keepdims=True))
        p = jnp.exp2((now - new_top) * SCALE).astype(jnp.bfloat16)
        shrink = jnp.exp2((top - new_top) * SCALE)
        off = pl.multiple_of(low_of(which) + tile * TILE, HEAD)
        acc[which] = acc[which] * shrink + mix(off, TILE, p)
        return new_top

    def begin_step(which, tiles, extra=()):
        for e in range(2):
            arrived(q.at[which, pl.ds(e * 64, 64)], q_recv.at[which, e])
        diag = pl.multiple_of(low_of(which) + 9 * TILE, HEAD)
        first = masked(weigh(which, diag, HEAD), allowed_at(which, diag, HEAD, True))
        jobs = [(which, tile) for tile in tiles] + list(extra)
        fill(0, which, tiles[0], True)
        top = jnp.max(first, axis=0, keepdims=True)
        acc[which] = mix(diag, HEAD, jnp.exp2((first - top) * SCALE).astype(jnp.bfloat16))
        for u, (one, tile) in enumerate(jobs):
            if u + 1 < len(jobs):
                fill((u + 1) % 2, *jobs[u + 1])
            if u == len(tiles):
                tops[which] = top
                top = tops[one]
            top = fold(u % 2, one, tile, top)
        tops[jobs[-1][0]] = top

    def end_step(n):
        which = step_of(n)
        then = step_of(jnp.minimum(n + 1, STEPS - 1))
        base = 3 - 2 * lax.rem(which, 2)
        top = tops[which]
        for u in range(5):
            if u < 4:
                fill(u % 2, which, base + u + 1)
            else:
                fill(2, then, 3 - 2 * lax.rem(then, 2))
            top = fold((u - 1) % 2 if u else 2, which, base + u, top)
        done = acc[which, :HEAD] / acc[which, HEAD:HEAD + 1]
        for g in range(GROUP):
            att_out[n, :, g * HEAD:(g + 1) * HEAD] = done[:, g * HEAD:(g + 1) * HEAD].T.astype(jnp.bfloat16)

    def give_back(n, e):
        which = step_of(n)
        t = 2 * lax.rem(which, 2) + e
        src = att_out.at[n, pl.ds(e * 64, 64)]
        dst = att.at[
            which // 2,
            pl.ds(pl.multiple_of(c * 64, 64), 64),
            pl.ds(pl.multiple_of((x // 2) * 512, 512), 512),
        ]
        recv = att_recv.at[which // 2, x // 2, c]
        copy = remote(src, dst, att_send.at[n, e], recv, at(t, lax.rem(x, 2)))
        return (t == x) & (lax.rem(x, 2) == c), copy, src, dst, recv

    def near(half, which):
        return remote(
            near_out.at[half, which], near_in.at[half, which],
            near_send.at[half, which], near_recv.at[half, which], sibling,
        )

    def cross(half):
        return remote(
            cross_out.at[half], cross_in.at[half], cross_send.at[half], cross_recv.at[half], facing
        )

    def quarter(half, k, into):
        col = pl.multiple_of(k * 1024, 1024)
        into(jnp.dot(att[half], w[:, pl.ds(col, 1024)], preferred_element_type=jnp.float32))

    def project(half):
        for e in range(2):
            for d in range(2):
                arrived(
                    att.at[half, pl.ds(d * 64, 64), pl.ds(e * 512, 512)], att_recv.at[half, e, d]
                )

        def to_near(which):
            def into(value):
                near_out[half, which] = value.astype(jnp.bfloat16)
            return into

        def to_part(value):
            part[half] = value

        def to_own(value):
            own[half] = value

        quarter(half, (1 - yl) * 2 + 1 - c, to_near(0))
        near(half, 0).start()
        quarter(half, (1 - yl) * 2 + c, to_part)
        quarter(half, yl * 2 + 1 - c, to_near(1))
        near(half, 1).start()
        quarter(half, yl * 2 + c, to_own)

    def combine(half):
        near(half, 0).wait_recv()
        cross_out[half] = (part[half] + near_in[half, 0].astype(jnp.float32)).astype(jnp.bfloat16)
        cross(half).start()

    def begin_far(a, carry):
        begin_step(2 * a + 1, (8, 7, 6))
        return carry

    def begin_near(a, carry):
        begin_step(2 * a, (8, 2, 1, 0), ((2 * a + 1, 0),))
        return carry

    lax.fori_loop(0, 2, begin_far, 0)
    pass_below(shards[2])
    pass_below(shards[3])
    lax.fori_loop(2, 4, begin_far, 0)
    from_sibling(0)
    lax.fori_loop(0, 2, begin_near, 0)
    for shard in shards:
        pass_across(shard)
    lax.fori_loop(2, 4, begin_near, 0)
    from_sibling(1)
    w_copy.wait()
    fill(2, step_of(0), 3 - 2 * lax.rem(step_of(0), 2))

    def turn(n, carry):
        end_step(n)
        for e in range(2):
            is_self, copy, src, dst, recv = give_back(n, e)
            each_way(is_self, copy, src, dst, recv)

        @pl.when((n == 4) | (n == 6))
        def _():
            combine(n // 2 - 2)

        @pl.when((n == 3) | (n == 5) | (n == 7))
        def _():
            project(n // 2 - 1)

        return carry

    lax.fori_loop(0, STEPS, turn, 0)
    combine(2)
    project(3)
    combine(3)

    def out_copy(half):
        rows = pl.ds(half * PART, PART)
        return pltpu.make_async_copy(out_loc.at[rows], out_hbm.at[rows], out_sem.at[half])

    for half in range(4):
        near(half, 1).wait_recv()
        cross(half).wait_recv()
        out_loc[half * PART:(half + 1) * PART, :] = (
            own[half] + near_in[half, 1].astype(jnp.float32) + cross_in[half].astype(jnp.float32)
        ).astype(jnp.bfloat16)
        out_copy(half).start()

    for is_self, copy in exchanged:
        @pl.when(jnp.logical_not(is_self))
        def _():
            copy.wait_send()

    for shard in range(4):
        to_above(shard).wait_send()
        to_across(0, shard).wait_send()
        for slot in range(3):
            to_sibling(slot, shard).wait_send()
    for n in range(STEPS):
        for e in range(2):
            is_self, copy, _, _, _ = give_back(n, e)

            @pl.when(jnp.logical_not(is_self))
            def _():
                copy.wait_send()

    for half in range(4):
        out_copy(half).wait()
        near(half, 0).wait_send()
        near(half, 1).wait_send()
        cross(half).wait_send()


def on_device(queries, keys, values, lengths, out_weight):
    bf16, f32 = jnp.bfloat16, jnp.float32
    dma = pltpu.SemaphoreType.DMA
    anywhere = pl.BlockSpec(memory_space=pl.ANY)
    return pl.pallas_call(
        kernel,
        out_shape=jax.ShapeDtypeStruct((ROWS, 1024), bf16),
        in_specs=[pl.BlockSpec(memory_space=pltpu.SMEM)] + [anywhere] * 4,
        out_specs=anywhere,
        scratch_shapes=[
            pltpu.VMEM((ROWS, 1024), bf16),
            pltpu.VMEM((ROWS, 256), bf16),
            pltpu.VMEM((2, ROWS, HEAD), bf16),
            pltpu.VMEM((1024, 4096), bf16),
            pltpu.VMEM((2, WINDOW, HEAD), bf16),
            pltpu.VMEM((STEPS, HEAD, 512), bf16),
            pltpu.VMEM((STEPS, HEAD), jnp.int32),
            pltpu.VMEM((3, TILE, 512), f32),
            pltpu.VMEM((STEPS, HEAD + 16, 512), f32),
            pltpu.VMEM((STEPS, 1, 512), f32),
            pltpu.VMEM((STEPS, HEAD, 512), bf16),
            pltpu.VMEM((4, PART, 1024), bf16),
            pltpu.VMEM((4, 2, PART, 1024), bf16),
            pltpu.VMEM((4, 2, PART, 1024), bf16),
            pltpu.VMEM((4, PART, 1024), bf16),
            pltpu.VMEM((4, PART, 1024), bf16),
            pltpu.VMEM((4, PART, 1024), f32),
            pltpu.VMEM((4, PART, 1024), f32),
            dma((2,)),
            dma((2, 2)), dma((4,)),
            dma((4, 2, 2)), dma((STEPS, 2)),
            dma((4,)), dma((4,)),
            dma((4,)), dma((4,)),
            dma((3, 4)), dma((3, 4)),
            dma((STEPS, 2)), dma((4, 2, 2)),
            dma((4, 2)), dma((4, 2)),
            dma((4,)), dma((4,)), dma((4,)),
        ],
        compiler_params=pltpu.CompilerParams(
            collective_id=0, has_side_effects=True, vmem_limit_bytes=56 * 2**20
        ),
        name="attend_and_project",
    )(lengths, queries, keys, values, out_weight)


def solution(mesh):
    in_specs = (P("seq", "head"), P("seq", "head"), P("seq", "head"), P(), P("head", None))
    return jax.shard_map(
        on_device, mesh=mesh, in_specs=in_specs, out_specs=P("seq", "head"), check_vma=False
    )
```
